32 devices in a mesh: slab: 2 (over y), row: 16 (over z, x, core).
Axes of the slice: x: 2, y: 2, z: 4, core: 2. Of those that a mesh axis runs over, the one named last changes fastest.
Arguments:
- calib: bfloat16 [2048, 8192], P('slab', 'row'), parts along dimension 0, may hold values from -6 to 6
- weights: bfloat16 [16384, 512], P(('slab', 'row')), parts along dimension 0, may hold values from -0.25 to 0.25
- hess_inv: float32 [16384, 8192], P(('slab', 'row')), parts along dimension 0, as said below
- block_scale: float32 [512, 512], P(('slab', 'row')), parts along dimension 0, may hold values from 0.04 to 0.4
Outputs:
- rounded: float32 [16384, 512], P(('slab', 'row')), parts along dimension 0
- dual: float32 [16384, 512], P(('slab', 'row')), parts along dimension 0
The draws below stay inside these ranges and needn't reach their ends.
There are 2 independent parts, one for each index of `slab`. The reference program is written for one: setup_inputs(seed, part) draws one part's arguments, and reference() takes and returns one part's arrays. A program takes and returns all parts, laid end to end along the dimension named above; each array names one. Nothing has to cross between parts.
Inputs may be any that keep to these rules, and one draw needn't show every extreme that they name: hess_inv is symmetric and positive definite.
All inputs are finite; a program needn't handle non-finite values.
Results may differ from the reference program's by a relative error of at most 0.011.
The reference program's roundings to bfloat16 on the way (of `outputs16` and `right`) count: a program that leaves them out, or rounds other values in their place, can miss the bound.
Values may be sent and summed in bfloat16 or wider, within the bound.
A program may use at most 64 MiB of HBM per device.

```python
import math
import jax
import jax.numpy as jnp
from jax import lax

K = 8192
C = 512
TOKENS = 1024
HB = 32
ITERS = 3


def draw_hess_inv(key, part):
    base = jax.random.fold_in(key, 11)
    first, second = jax.random.split(base)
    noise = jax.random.normal(first, (K, K), jnp.float32)
    middle = jax.random.uniform(second, (K,), jnp.float32, 0.6, 1.2)
    spread = jnp.float32(0.25 / math.sqrt(2.0 * K))
    return jnp.diag(middle) + (noise + noise.T) * spread


def level_of(own_key, dims, pieces, least, largest):
    gain, own = 1.0, jax.random.fold_in(own_key, 6)
    for position, blocks in pieces:
        draws = jnp.exp(jax.random.uniform(jax.random.fold_in(own, position), (blocks,), jnp.float32, least / len(pieces), largest / len(pieces)))
        gain = gain * jnp.repeat(draws, dims[position] // blocks).reshape([-1 if axis == position else 1 for axis in range(len(dims))])
    return gain


def scatter_about(stream_key, dims, deviation, bound, cuts=(), held_as=jnp.bfloat16):
    loudness = level_of(stream_key, dims, cuts, -0.22, 0.18) if cuts else 1.0
    array = jax.random.normal(stream_key, dims, jnp.float32) * deviation * loudness
    return jnp.minimum(jnp.maximum(array, -bound), bound).astype(held_as)


def setup_inputs(seed: int = 0, part: int = 0) -> dict:
    streams_of = jax.random.split(jax.random.key(seed), 5)
    own_keys = jax.random.split(jax.random.fold_in(streams_of[4], part), 5)
    return {
        "calib": scatter_about(own_keys[0], (TOKENS, K), 1.0, 6.0, ((1, 16),)),
        "weights": jnp.clip(jax.random.uniform(own_keys[1], (K, C), jnp.float32, -0.25, 0.25) * level_of(own_keys[1], (K, C), ((0, 16),), -0.4, 0.0), -0.25, 0.25).astype(jnp.bfloat16),
        "hess_inv": draw_hess_inv(jax.random.fold_in(jax.random.fold_in(streams_of[4], part), 71), part),
        "block_scale": jnp.clip(jnp.exp(math.log(0.4) - 2.3025851 * jax.random.uniform(own_keys[3], (K // HB, C), jnp.float32) ** level_of(own_keys[3], (K // HB, C), ((0, 16),), -0.2, 0.2)), 0.04, 0.4),
    }


def hadamard_table(width):
    index = jnp.arange(width, dtype=jnp.int32)
    left = index[:, None]
    right = index[None, :]
    parity = jnp.zeros((width, width), jnp.int32)
    for bit in range(width.bit_length() - 1):
        parity = parity + jnp.bitwise_and(jnp.right_shift(left, bit), 1) * jnp.bitwise_and(jnp.right_shift(right, bit), 1)
    signs = jnp.where(parity % 2 == 0, 1.0, -1.0).astype(jnp.float32)
    return signs * jnp.float32(1.0 / math.sqrt(width))

def blockwise(values, table):
    rows, cols = values.shape
    width = table.shape[0]
    blocks = values.reshape(rows // width, width, cols)
    spun = jnp.einsum('ij,bjc->bic', table, blocks, precision=lax.Precision.HIGHEST)
    return spun.reshape(rows, cols)

def project(solved, dual, scale, table):
    width = table.shape[0]
    rows, cols = solved.shape
    spun = blockwise(solved + dual, table).reshape(rows // width, width, cols)
    shares = scale[:, None, :]
    ratio = spun / shares
    snapped = shares * (ratio - jnp.sin(2.0 * math.pi * ratio) / (4.0 * math.pi))
    return blockwise(snapped.reshape(rows, cols), table)

def reference(calib, weights, hess_inv, block_scale):
    table = hadamard_table(HB)
    outputs = jnp.dot(calib, weights, preferred_element_type=jnp.float32)
    outputs16 = outputs.astype(jnp.bfloat16)
    factor = jnp.float32(0.25 / math.sqrt(K * TOKENS))
    target = lax.dot_general(calib, outputs16, (((0,), (0,)), ((), ())), preferred_element_type=jnp.float32) * factor
    current = weights.astype(jnp.float32)
    dual = jnp.zeros_like(current)
    for step in range(ITERS):
        right = (target + 0.5 * (current - dual)).astype(jnp.bfloat16)
        solved = jnp.dot(hess_inv, right.astype(jnp.float32), precision=lax.Precision.HIGHEST)
        fresh = project(solved, dual, block_scale, table)
        dual = dual + solved - fresh
        current = fresh
    return (current, dual)
```

```python
import functools
import math

import jax
import jax.numpy as jnp
import numpy as np
from jax import lax
from jax.experimental import pallas as pl
from jax.experimental.pallas import tpu as pltpu
from jax.sharding import PartitionSpec as P

HB = 32
ITERS = 3
MESH = pl.DeviceIdType.MESH
F32 = jnp.float32
BF16 = jnp.bfloat16

SIN = (6.283185306817099, -41.34170217065974, 81.60524536030235, -76.70576095162302, 42.057370069229776, -15.084554763275257, 3.7759575477344116, -0.6150599564076469)


def grid_of(n):
    chips = n // 2
    nx = 2 ** ((chips.bit_length() - 1) // 3)
    return chips // nx, nx


def hadamard_signs(size):
    i = np.arange(size)
    common = (i[:, None] & i[None, :]) % HB
    parity = np.zeros((size, size), np.int64)
    for bit in range(HB.bit_length() - 1):
        parity += (common >> bit) & 1
    signs = np.where(parity % 2 == 0, 1.0, -1.0)
    same = (i[:, None] // HB) == (i[None, :] // HB)
    return np.where(same, signs, 0.0)


def dot(a, b):
    return jnp.dot(a, b, preferred_element_type=F32)


def spin(signs, values):
    high = values.astype(BF16)
    low = (values - high.astype(F32)).astype(BF16)
    return (dot(signs, high) + dot(signs, low)) * F32(1.0 / math.sqrt(HB))


def snap(spun, scale):
    t = spun / scale
    f = t - jnp.floor(t + 0.5)
    f2 = f * f
    p = jnp.full_like(f, SIN[-1])
    for c in SIN[-2::-1]:
        p = p * f2 + F32(c)
    return spun - scale * (f * p) * F32(1.0 / (4.0 * math.pi))


def admm_kernel(
    nz, nx, chunk,
    target_ref, weights_ref, hess_ref, scale_ref, signs_ref,
    cur_ref, dual_ref,
    held, h16, hlow, stage, acc, stage_sem, send_sem, recv_sem,
):
    nb = 2 * nz * nx
    rows = weights_ref.shape[0]
    slab = lax.axis_index("slab")
    me = lax.axis_index("row")
    core = lax.rem(me, 2)
    x = lax.rem(me // 2, nx)
    z = me // (2 * nx)

    def at(zz, xx, cc):
        return (zz * nx + xx) * 2 + cc

    has = (z + 1 < nz, z >= 1, x + 1 < nx, x >= 1, None)
    peer = (
        at(z + 1, x, core), at(z - 1, x, core),
        at(z, x + 1, core), at(z, x - 1, core), at(z, x, 1 - core),
    )
    barrier = pltpu.get_barrier_semaphore()

    def maybe(cond, fn):
        if cond is None:
            fn()
        else:
            pl.when(cond)(fn)

    def greet(kind):
        def go():
            pl.semaphore_signal(barrier, inc=1, device_id=(slab, peer[kind]), device_id_type=MESH)
        return go

    for kind in range(5):
        maybe(has[kind], greet(kind))
    pl.semaphore_wait(barrier, 1 + sum(h.astype(jnp.int32) for h in has[:4]))

    def copy(it, kind, blk):
        return pltpu.make_async_remote_copy(
            src_ref=held.at[it, blk], dst_ref=held.at[it, blk],
            send_sem=send_sem.at[kind, blk], recv_sem=recv_sem.at[it, blk],
            device_id=(slab, peer[kind]), device_id_type=MESH,
        )

    def send(it, kind, blk):
        maybe(has[kind], lambda: copy(it, kind, blk).start())

    def arrived(it, blk):
        copy(it, 4, blk).wait_recv()

    cur_ref[...] = weights_ref[...].astype(F32)
    dual_ref[...] = jnp.zeros_like(dual_ref)

    cols = hess_ref.shape[1]
    n_chunks = cols // chunk

    def fetch(i):
        slot = lax.rem(i, 2)
        off = pl.multiple_of(i * chunk, chunk)
        return pltpu.make_async_copy(hess_ref.at[:, pl.ds(off, chunk)], stage.at[slot], stage_sem.at[slot])

    def load_hess():
        fetch(0).start()

        def body(i, carry):
            @pl.when(i + 1 < n_chunks)
            def _():
                fetch(i + 1).start()

            fetch(i).wait()
            slot = lax.rem(i, 2)
            for j in range(chunk // rows):
                b = i * (chunk // rows) + j
                h16[b] = stage[slot, :, j * rows:(j + 1) * rows].astype(BF16)

                @pl.when(b == me)
                def _():
                    v = stage[slot, :, j * rows:(j + 1) * rows]
                    hlow[...] = (v - v.astype(BF16).astype(F32)).astype(BF16)
            return carry

        lax.fori_loop(0, n_chunks, body, 0)

    group = signs_ref.shape[0]

    def iteration(it, carry):
        held[it, me] = (target_ref[...] + 0.5 * (cur_ref[...] - dual_ref[...])).astype(BF16)
        for kind in (0, 1, 2, 3, 4):
            send(it, kind, me)

        @pl.when(it == 0)
        def _():
            load_hess()

        acc[...] = dot(hlow[...], held[it, me])

        def step(s, c0):
            for sign in (-1, 1):
                zz = z + sign * s

                @pl.when((zz >= 0) & (zz < nz))
                def _():
                    blk = at(zz, x, core)
                    arrived(it, blk)
                    send(it, 0 if sign < 0 else 1, blk)
                    for kind in (2, 3, 4):
                        send(it, kind, blk)

            for sign in (-1, 1):
                zz = z + sign * (s - 1)
                ok = (zz >= 0) & (zz < nz)
                if sign > 0:
                    ok = ok & (s > 1)
                for t in range(1, nx):
                    for side in (-1, 1):
                        xx = x + side * t

                        @pl.when(ok & (xx >= 0) & (xx < nx))
                        def _():
                            blk = at(zz, xx, core)
                            arrived(it, blk)
                            if nx > 2:
                                send(it, 2 if side < 0 else 3, blk)
                            send(it, 4, blk)

            def part(q, c1):
                other = q // (2 * nx)
                u = s - 1 - other
                sign = lax.rem(q, 2) * 2 - 1
                xx = lax.rem(q // 2, nx)
                zz = z + sign * u

                @pl.when((zz >= 0) & (zz < nz) & (u >= 0) & ((u > 0) | (sign < 0)))
                def _():
                    cc = core + other * (1 - 2 * core)
                    blk = at(zz, xx, cc)

                    @pl.when(other == 1)
                    def _():
                        arrived(it, blk)

                    acc[...] += dot(h16[blk], held[it, blk])
                return c1

            return lax.fori_loop(0, 4 * nx, part, c0)

        lax.fori_loop(1, nz + 2, step, 0)

        for g in range(rows // group):
            part = pl.ds(g * group, group)
            moved = acc[part] + dual_ref[part]
            spun = spin(signs_ref[...], moved).reshape(group // HB, HB, -1)
            scale = scale_ref[g * (group // HB):(g + 1) * (group // HB)][:, None, :]
            snapped = snap(spun, scale).reshape(group, -1)
            fresh = spin(signs_ref[...], snapped)
            dual_ref[part] = moved - fresh
            cur_ref[part] = fresh

        def gone(q, c0):
            zz = q // nx
            xx = lax.rem(q, nx)
            blk = at(zz, xx, core)

            def wait(kind):
                return lambda: copy(it, kind, blk).wait_send()

            pl.when((xx == x) & (zz <= z) & (z + 1 < nz))(wait(0))
            pl.when((xx == x) & (zz >= z) & (z >= 1))(wait(1))
            pl.when((xx <= x) & (x + 1 < nx))(wait(2))
            pl.when((xx >= x) & (x >= 1))(wait(3))
            wait(4)()
            return c0

        lax.fori_loop(0, nz * nx, gone, 0)
        return carry

    lax.fori_loop(0, ITERS, iteration, 0)


def admm(n, target, weights, hess_inv, block_scale):
    nz, nx = grid_of(n)
    rows, cols = weights.shape
    order = hess_inv.shape[1]
    chunk = max(rows, 512)
    group = min(rows, 256)
    signs = jnp.asarray(hadamard_signs(group), BF16)
    vmem = pl.BlockSpec(memory_space=pltpu.VMEM)
    return pl.pallas_call(
        functools.partial(admm_kernel, nz, nx, chunk),
        out_shape=[jax.ShapeDtypeStruct((rows, cols), F32)] * 2,
        in_specs=[vmem, vmem, pl.BlockSpec(memory_space=pl.ANY), vmem, vmem],
        out_specs=[vmem, vmem],
        scratch_shapes=[
            pltpu.VMEM((ITERS, n, rows, cols), BF16),
            pltpu.VMEM((n, rows, rows), BF16),
            pltpu.VMEM((rows, rows), BF16),
            pltpu.VMEM((2, rows, chunk), F32),
            pltpu.VMEM((rows, cols), F32),
            pltpu.SemaphoreType.DMA((2,)),
            pltpu.SemaphoreType.DMA((5, n)),
            pltpu.SemaphoreType.DMA((ITERS, n)),
        ],
        compiler_params=pltpu.CompilerParams(
            collective_id=0, has_side_effects=True, vmem_limit_bytes=56 * 1024 * 1024
        ),
        cost_estimate=pl.CostEstimate(
            flops=2 * ITERS * rows * order * cols, bytes_accessed=4 * rows * order, transcendentals=0
        ),
    )(target, weights, hess_inv, block_scale, signs)


def body(n, order, calib, weights, hess_inv, block_scale):
    partial_out = jnp.dot(calib, weights, preferred_element_type=F32)
    outputs16 = lax.psum(partial_out, "row").astype(BF16)
    factor = F32(0.25 / math.sqrt(order * calib.shape[0]))
    target = (
        lax.dot_general(calib, outputs16, (((0,), (0,)), ((), ())), preferred_element_type=F32)
        * factor
    )
    return tuple(admm(n, target, weights, hess_inv, block_scale))


def solution(mesh):
    n = mesh.shape["row"]
    in_specs = (
        P("slab", "row"),
        P(("slab", "row"), None),
        P(("slab", "row"), None),
        P(("slab", "row"), None),
    )
    out_specs = (P(("slab", "row"), None), P(("slab", "row"), None))

    def run(calib, weights, hess_inv, block_scale):
        inner = functools.partial(body, n, hess_inv.shape[1])
        return jax.shard_map(
            inner, mesh=mesh, in_specs=in_specs, out_specs=out_specs, check_vma=False
        )(calib, weights, hess_inv, block_scale)

    return run
```
